32 devices in a mesh: groups: 2 (over y), adapters: 4 (over z), tp: 2 (over x), sub: 2 (over core).
Axes of the slice: x: 2, y: 2, z: 4, core: 2. Of those that a mesh axis runs over, the one named last changes fastest.
Arguments:
- tokens: bfloat16 [16384, 8192], P(('groups', 'adapters', 'sub'), 'tp'), parts along dimension 0, may hold values from -6 to 6
- token_adapter_index: int32 [16384, 1], P(('groups', 'adapters', 'sub')), parts along dimension 0, may hold values from 0 to 31; in each aligned block of 1024 rows (0 to 1023, 1024 to 2047, ...) at most 64 rows name the same one
- adapter_slot_table: int32 [32], replicated, may hold values from 0 to 31, each once
- base_value_matrix: bfloat16 [8192, 1024], P(None, 'tp'), may hold values from -0.0625 to 0.0625
- adapter_down_weight: bfloat16 [32, 8192, 64], P(('adapters', 'sub'), 'tp'), may hold values from -0.0625 to 0.0625
- adapter_up_weight: bfloat16 [32, 64, 1024], P(('adapters', 'sub'), None, 'tp'), may hold values from -0.75 to 0.75
- adapter_scale_rows: float32 [32], P(('adapters', 'sub')), may hold values from 0.5 to 2
Outputs:
- values: bfloat16 [16384, 1024], P(('groups', 'adapters', 'sub'), 'tp'), parts along dimension 0
The draws below stay inside these ranges and needn't reach their ends.
There are 2 independent parts, one for each index of `groups`. The reference program is written for one: setup_inputs(seed, part) draws one part's arguments, and reference() takes and returns one part's arrays. A program takes and returns all parts, laid end to end along the dimension named above; an argument that names none is the same for every part. Nothing has to cross between parts.
Inputs may be any that keep to these rules, and one draw needn't show every extreme that they name: `token_adapter_index`: in each aligned block of 1024 rows (the rows of one index of adapters and sub) no adapter is named by more than 64 rows, a bound that some block reaches; every adapter is named somewhere. `adapter_slot_table`: A permutation: every stored row is used by exactly one adapter.
All inputs are finite; a program needn't handle non-finite values.
Results may differ from the reference program's by a relative error of at most 0.0051.
Values may be sent and summed in bfloat16 or wider, within the bound.
A program may use at most 192 MiB of HBM per device.

```python
import math
import jax
import jax.numpy as jnp
import numpy as np
from jax import lax

MODEL_WIDTH = 8192
VALUE_WIDTH = 1024
ADAPTER_RANK = 64
TOK_GRP = 1024
ADAPTER_TOTAL = 32
CAP = 64
TOKENS = 8192


def level_of(key, extent, shards, low, largest):
    def one(dim, parts):
        steps = jax.random.uniform(jax.random.fold_in(jax.random.fold_in(key, 6), dim), (parts,), jnp.float32, low / len(shards), largest / len(shards))
        return jnp.repeat(jnp.exp(steps), extent[dim] // parts).reshape((-1,) + (1,) * (len(extent) - dim - 1))

    factor_of = one(*shards[0])
    for cut in shards[1:]:
        factor_of = factor_of * one(*cut)
    return factor_of


def deal_out(own_key, own, number, rows, amount, top, bound, lean):
    order = jax.random.permutation(own_key, amount)
    crowded, common = load_shares(amount, rows * top, bound, lean, True), load_shares(amount, rows * top, bound, lean, False)
    places = jnp.arange(amount)

    def named(sizes, offset_by):
        used = int((sizes > 0).sum())
        fixed = max(1, used // 4)
        moved = fixed + (places - fixed + offset_by * (used - fixed)) % max(1, amount - fixed)
        return jnp.zeros((amount,), jnp.int32).at[order[jnp.where(places < fixed, places, moved)]].set(jnp.asarray(sizes, jnp.int32))

    sizes = jnp.where(number % 4 == 0, named(crowded, number // 4), named(common, number - number // 4 - 1))
    mixed = jax.random.permutation(jax.random.fold_in(own, 3), amount)
    giver, taker = mixed[0:amount // 2 * 2:2], mixed[1:amount // 2 * 2:2]
    margin = jnp.minimum(sizes[giver] - 1, bound - sizes[taker]) // 2
    margin = jnp.where((giver == order[0]) | (taker == order[0]) | (sizes[taker] == 0), 0, jnp.maximum(margin, 0))
    moved = jax.random.randint(jax.random.fold_in(own, 4), (amount // 2,), 0, 1 << 20) % (margin + 1)
    sizes = sizes.at[giver].add(-moved).at[taker].add(moved)
    items = jnp.searchsorted(jnp.cumsum(sizes), jnp.arange(rows * top), side="right").astype(jnp.int32)
    listing = items.reshape(top, rows).T
    listing = listing[jax.random.permutation(jax.random.fold_in(own, 1), rows)]
    offset_by = jax.random.randint(jax.random.fold_in(own, 2), (rows, 1), 0, top)
    return jnp.take_along_axis(listing, (jnp.arange(top)[None, :] + offset_by) % top, axis=1)


def load_shares(count, total, limit, lean, full):
    weights = [(1 << 20) // math.isqrt(rank ** lean) + 1 for rank in range(1, count + 1)]
    largest = limit if full else min(limit, max(-(-total // count), total * weights[0] // sum(weights)))
    least = 1 if total - largest >= count - 1 else 0
    counts, spare = [largest] + [least] * (count - 1), total - largest - least * (count - 1)
    while spare > 0:
        movable = [i for i in range(1, count) if counts[i] < largest] or [i for i in range(1, count) if counts[i] < limit]
        pool, left = sum([weights[i] for i in movable]), spare
        for i in movable:
            extra = min(limit - counts[i], max(1, left * weights[i] // pool), spare)
            counts[i] = counts[i] + extra
            spare = spare - extra
    return np.array(counts)


def noise(key, dims, spread, reach, shards=(), held_as=jnp.bfloat16):
    factor_of = level_of(key, dims, shards, -0.22, 0.18) if shards else 1.0
    entries = jax.random.normal(key, dims, jnp.float32) * spread * factor_of
    return jnp.minimum(jnp.maximum(entries, -reach), reach).astype(held_as)


def setup_inputs(seed: int = 0, part: int = 0) -> dict:
    streams_of = jax.random.split(jax.random.key(seed), 8)
    part_keys = jax.random.split(jax.random.fold_in(streams_of[7], part), 8)
    tokens = noise(part_keys[0], (TOKENS, MODEL_WIDTH), 1.0, 6.0, ((0, 8), (1, 2)))
    token_adapter_index_keys = jax.random.split(jax.random.fold_in(part_keys[1], 1), TOKENS // TOK_GRP)
    token_adapter_index_turns = jax.random.permutation(jax.random.fold_in(part_keys[1], 3), TOKENS // TOK_GRP)
    token_adapter_index = jax.vmap(lambda own, number: deal_out(jax.random.fold_in(part_keys[1], 2), own, number, TOK_GRP, ADAPTER_TOTAL, 1, CAP, 2))(token_adapter_index_keys, token_adapter_index_turns).reshape((TOKENS, 1))
    adapter_slot_table = jax.random.permutation(streams_of[2], ADAPTER_TOTAL).astype(jnp.int32)
    base_value_matrix = noise(streams_of[3], (MODEL_WIDTH, VALUE_WIDTH), MODEL_WIDTH ** -0.5, 0.0625, ((1, 2),))
    adapter_down_weight = noise(streams_of[4], (ADAPTER_TOTAL, MODEL_WIDTH, ADAPTER_RANK), MODEL_WIDTH ** -0.5, 0.0625, ((0, 8), (1, 2)))
    adapter_up_weight = noise(streams_of[5], (ADAPTER_TOTAL, ADAPTER_RANK, VALUE_WIDTH), ADAPTER_RANK ** -0.5, 0.75, ((0, 8), (2, 2)))
    adapter_scale_rows = jnp.clip(jnp.exp(math.log(2.0) - 1.3862944 * jax.random.uniform(streams_of[6], (ADAPTER_TOTAL,), jnp.float32) ** level_of(streams_of[6], (ADAPTER_TOTAL,), ((0, 8),), -0.2, 0.2)), 0.5, 2.0)
    return {"tokens": tokens, "token_adapter_index": token_adapter_index, "adapter_slot_table": adapter_slot_table, "base_value_matrix": base_value_matrix, "adapter_down_weight": adapter_down_weight, "adapter_up_weight": adapter_up_weight, "adapter_scale_rows": adapter_scale_rows}


def reference(tokens, token_adapter_index, adapter_slot_table, base_value_matrix, adapter_down_weight, adapter_up_weight, adapter_scale_rows):
    adapter_count = adapter_slot_table.shape[0]
    stored_slot = adapter_slot_table[token_adapter_index[:, 0]].astype(jnp.int32)
    base_sum = jnp.dot(tokens, base_value_matrix, preferred_element_type=jnp.float32)
    sort_order = jnp.argsort(stored_slot, stable=True).astype(jnp.int32)
    inverse = jnp.argsort(sort_order, stable=True).astype(jnp.int32)
    slot_iota = jnp.arange(adapter_count, dtype=jnp.int32)
    slot_counts = jnp.sum((stored_slot[:, None] == slot_iota[None, :]).astype(jnp.int32), axis=0).astype(jnp.int32)
    offsets = (jnp.cumsum(slot_counts) - slot_counts).astype(jnp.int32)
    longest = (TOKENS // TOK_GRP) * CAP
    padded = jnp.concatenate([tokens[sort_order], jnp.zeros((longest, tokens.shape[1]), tokens.dtype)], axis=0)

    def per_adapter(token_index):
        incoming_rows = lax.dynamic_slice_in_dim(padded, offsets[token_index].astype(jnp.int32), longest, 0)
        rank_product = jnp.dot(incoming_rows, adapter_down_weight[token_index], preferred_element_type=jnp.float32).astype(jnp.bfloat16)
        lowrank_delta_rows = jnp.dot(rank_product, adapter_up_weight[token_index], preferred_element_type=jnp.float32)
        return (lowrank_delta_rows * adapter_scale_rows[token_index]).astype(jnp.bfloat16)

    deltas = lax.map(per_adapter, slot_iota)
    slot_rank = (inverse - offsets[stored_slot]).astype(jnp.int32)
    own_delta = deltas[stored_slot, slot_rank]
    return (base_sum + own_delta.astype(jnp.float32)).astype(jnp.bfloat16)
```

```python
import functools

import jax
import jax.numpy as jnp
from jax import lax
from jax.experimental import pallas as pl
from jax.experimental.pallas import tpu as pltpu
from jax.sharding import PartitionSpec as P

LANES = 128
PARTS = 4


def kernel(
    depth,
    tok_hbm, base_hbm, down_hbm, up_hbm, key_ref,
    out_ref,
    tok, wmine, wcross, buf, acc, pout, pin, lacc, sacc, lpo, lpi,
    local_sem, send_z, recv_z, send_y, recv_y, send_c, recv_c, send_x, recv_x,
):
    rows, feats = tok.shape
    held_rows = buf.shape[1]
    outs = wmine.shape[1]
    half_outs = outs // 2
    half_feats = feats // 2
    half = held_rows // 2
    step_rows = half // PARTS
    tile = min(512, rows)
    g = lax.axis_index("groups")
    z = lax.axis_index("adapters")
    p = lax.axis_index("tp")
    s = lax.axis_index("sub")
    me = 2 * z + s

    def remote(src, dst, send, recv, to):
        return pltpu.make_async_remote_copy(
            src_ref=src, dst_ref=dst, send_sem=send, recv_sem=recv,
            device_id=to, device_id_type=pl.DeviceIdType.MESH,
        )

    def piece(owner, h, q):
        start = pl.multiple_of(h * half + q * step_rows, step_rows)
        return buf.at[owner, pl.ds(start, step_rows)]

    def source(d, k):
        return z - k if d == 0 else z + k

    def exists(d, k):
        return z >= k if d == 0 else z + k < depth

    def can_send(d):
        return z + 1 < depth if d == 0 else z >= 1

    x_to, y_to, c_to = {"tp": 1 - p}, {"groups": 1 - g}, {"sub": 1 - s}

    def z_copy(d, k, q):
        block = piece(2 * source(d, k) + s, g, q)
        to = {"adapters": z + 1 if d == 0 else z - 1}
        return remote(block, block, send_z.at[d, k, q], recv_z.at[d, k, q], to)

    def z_arrival(d, k, q):
        block = piece(2 * source(d, k + 1) + s, g, q)
        return remote(block, block, send_z.at[d, k, q], recv_z.at[d, k, q], x_to)

    def y_copy(d, k, q, h):
        block = piece(2 * source(d, k + 1) + s, h, q)
        return remote(block, block, send_y.at[d, k, q], recv_y.at[d, k, q], y_to)

    def c_copy(d, k, q, w, core):
        block = piece(2 * source(d, k + 1) + core, g if w == 0 else 1 - g, q)
        return remote(block, block, send_c.at[d, k, q, w], recv_c.at[d, k, q, w], c_to)

    def own_copy(core):
        block = buf.at[2 * z + core]
        return remote(block, block, send_x.at[0], recv_x.at[0], c_to)

    def x_copy(c):
        first = pl.multiple_of((1 - p) * feats + s * half_feats, half_feats)
        return remote(
            base_hbm.at[pl.ds(first, half_feats), pl.ds(c * half_outs, half_outs)],
            wcross.at[c, pl.ds(pl.multiple_of(s * half_feats, half_feats), half_feats)],
            send_x.at[1 + c], recv_x.at[1 + c], x_to,
        )

    def xc_copy(c, core):
        block = wcross.at[c, pl.ds(pl.multiple_of(core * half_feats, half_feats), half_feats)]
        return remote(block, block, send_x.at[3 + c], recv_x.at[3 + c], c_to)

    def part_copy(c):
        return remote(pout.at[c], pin.at[c], send_x.at[5 + c], recv_x.at[5 + c], x_to)

    def low_copy():
        return remote(lpo, lpi, send_x.at[7], recv_x.at[7], x_to)

    loads = [
        pltpu.make_async_copy(down_hbm, buf.at[me, :, pl.ds(0, feats)], local_sem.at[0]),
        pltpu.make_async_copy(up_hbm, buf.at[me, :, pl.ds(feats, outs + LANES)], local_sem.at[1]),
        pltpu.make_async_copy(tok_hbm, tok, local_sem.at[2]),
        pltpu.make_async_copy(
            base_hbm.at[pl.ds(pl.multiple_of(p * feats, feats), feats)], wmine, local_sem.at[3]
        ),
    ]
    for load in loads:
        load.start()

    barrier = pltpu.get_barrier_semaphore()
    for to in (x_to, y_to, c_to):
        pl.semaphore_signal(barrier, inc=1, device_id=to, device_id_type=pl.DeviceIdType.MESH)
    for d in range(2):
        @pl.when(can_send(d))
        def _(d=d):
            to = {"adapters": z + 1 if d == 0 else z - 1}
            pl.semaphore_signal(barrier, inc=1, device_id=to, device_id_type=pl.DeviceIdType.MESH)
    pl.semaphore_wait(barrier, 3 + (z >= 1).astype(jnp.int32) + (z + 1 < depth).astype(jnp.int32))

    for c in range(2):
        x_copy(c).start()
    loads[0].wait()
    loads[1].wait()
    for q in range(PARTS):
        for d in range(2):
            @pl.when(can_send(d))
            def _(d=d, q=q):
                z_copy(d, 0, q).start()
    own_copy(s).start()

    def project(owner):
        @pl.loop(0, rows // tile)
        def _(i):
            at = pl.ds(pl.multiple_of(i * tile, tile), tile)
            wide = lax.dot_general(
                tok[at], buf[owner, :, pl.ds(0, feats)], (((1,), (1,)), ((), ())),
                preferred_element_type=jnp.float32,
            )
            key = key_ref[at]
            first, second = key == 4 * owner, key == 4 * owner + 2
            lacc[at] += jnp.where(first, wide[:, :LANES], 0.0) + jnp.where(second, wide[:, LANES:], 0.0)
            ones = jnp.concatenate(
                [jnp.where(first, 1.0, 0.0), jnp.where(second, 1.0, 0.0)], axis=1
            ).astype(jnp.bfloat16)
            sacc[at] += jnp.dot(
                ones, buf[owner, :, pl.ds(feats + outs, LANES)], preferred_element_type=jnp.float32
            )

    def z_events(k, q):
        for d in range(2):
            @pl.when(exists(d, k + 1))
            def _(d=d):
                z_arrival(d, k, q).wait_recv()
                if k + 1 < depth - 1:
                    @pl.when(can_send(d))
                    def _():
                        z_copy(d, k + 1, q).start()
                y_copy(d, k, q, g).start()
                c_copy(d, k, q, 0, s).start()

    def y_events(k, q):
        for d in range(2):
            @pl.when(exists(d, k + 1))
            def _(d=d):
                y_copy(d, k, q, 1 - g).wait_recv()
                c_copy(d, k, q, 1, s).start()

    def owners(d, k):
        @pl.when(exists(d, k + 1))
        def _():
            for q in range(PARTS):
                for w in range(2):
                    c_copy(d, k, q, w, 1 - s).wait_recv()

            @pl.loop(0, 2)
            def _(core):
                project(2 * source(d, k + 1) + core)

    def take_cross(c):
        x_copy_in = remote(
            wcross.at[c, pl.ds(pl.multiple_of(s * half_feats, half_feats), half_feats)],
            wcross.at[c, pl.ds(pl.multiple_of(s * half_feats, half_feats), half_feats)],
            send_x.at[1 + c], recv_x.at[1 + c], x_to,
        )
        x_copy_in.wait_recv()
        xc_copy(c, s).start()

    def cross(c):
        xc_copy(c, 1 - s).wait_recv()

        @pl.loop(0, rows // tile)
        def _(i):
            at = pl.ds(pl.multiple_of(i * tile, tile), tile)
            pout[c, at] = jnp.dot(
                tok[at], wcross[c], preferred_element_type=jnp.float32
            ).astype(jnp.bfloat16)

        part_copy(c).start()

    lacc[...] = jnp.zeros_like(lacc)
    sacc[...] = jnp.zeros_like(sacc)
    loads[2].wait()
    project(me)
    loads[3].wait()

    @pl.loop(0, rows // tile)
    def _(i):
        at = pl.ds(pl.multiple_of(i * tile, tile), tile)
        for c in range(2):
            cols = pl.ds(c * half_outs, half_outs)
            acc[at, cols] = jnp.dot(tok[at], wmine[:, cols], preferred_element_type=jnp.float32)

    def sibling():
        own_copy(1 - s).wait_recv()
        project(2 * z + 1 - s)

    steps = (depth - 1) * PARTS
    tasks = {1: [sibling], 3: [lambda: take_cross(0)], 4: [lambda: cross(0)],
             7: [lambda: take_cross(1)], 8: [lambda: cross(1)]}
    for k in range(depth - 1):
        tasks.setdefault(k * PARTS + PARTS + 1, []).append(lambda k=k: owners(0, k))
        tasks.setdefault(k * PARTS + PARTS + 2, []).append(lambda k=k: owners(1, k))
    for i in range(max(steps, max(tasks)) + 1):
        if i < steps:
            z_events(i // PARTS, i % PARTS)
        if 0 < i <= steps:
            y_events((i - 1) // PARTS, (i - 1) % PARTS)
        for task in tasks.get(i, []):
            task()

    folded = lacc[...] + pltpu.roll(lacc[...], LANES // 2, 1)
    low_lane = lax.broadcasted_iota(jnp.int32, lpo.shape, 1) < LANES // 2
    lpo[...] = jnp.where(low_lane, folded[: rows // 2], folded[rows // 2 :])
    low_copy().start()
    for c in range(2):
        part_copy(c).wait_recv()
    low_copy().wait_recv()
    both = lpo[...] + lpi[...]
    turned = pltpu.roll(both, LANES // 2, 1)
    lacc[pl.ds(0, rows // 2)] = jnp.where(low_lane, both, turned)
    lacc[pl.ds(rows // 2, rows // 2)] = jnp.where(low_lane, turned, both)

    end_tile = min(256, rows)

    @pl.loop(0, rows // end_tile)
    def _(i):
        at = pl.ds(pl.multiple_of(i * end_tile, end_tile), end_tile)
        low = lacc[at].astype(jnp.bfloat16).astype(jnp.float32)
        key = key_ref[at]
        spread = jnp.concatenate(
            [jnp.where(key == 2 * j, low, 0.0).astype(jnp.bfloat16) for j in range(4 * depth)], axis=1
        )
        scale = sacc[at]
        for c in range(2):
            cols = pl.ds(c * half_outs, half_outs)
            ups = buf[:, :, pl.ds(feats + c * half_outs, half_outs)].reshape(-1, half_outs)
            delta = jnp.dot(spread, ups, preferred_element_type=jnp.float32)
            wide_scale = jnp.concatenate([scale] * (half_outs // LANES), axis=1)
            delta = (delta * wide_scale).astype(jnp.bfloat16).astype(jnp.float32)
            base = acc[at, cols] + pin[c, at].astype(jnp.float32)
            out_ref[at, cols] = (base + delta).astype(jnp.bfloat16)

    for c in range(2):
        x_copy(c).wait_send()
        xc_copy(c, s).wait_send()
        part_copy(c).wait_send()
    low_copy().wait_send()
    own_copy(s).wait_send()
    for k in range(depth - 1):
        for d in range(2):
            @pl.when(exists(d, k) & can_send(d))
            def _(d=d, k=k):
                for q in range(PARTS):
                    z_copy(d, k, q).wait_send()

            @pl.when(exists(d, k + 1))
            def _(d=d, k=k):
                for q in range(PARTS):
                    y_copy(d, k, q, g).wait_send()
                    for w in range(2):
                        c_copy(d, k, q, w, s).wait_send()


def fused(depth, tokens, stored, base, down_rows, up_rows, scale_rows):
    rows, feats = tokens.shape
    held_rows, outs = up_rows.shape
    rank = held_rows // scale_rows.shape[0]
    high = lax.reduce_precision(scale_rows, 8, 7)
    mid = lax.reduce_precision(scale_rows - high, 8, 7)
    rest = scale_rows - high - mid
    place = jnp.arange(rank)[None, :]
    split = jnp.where(
        place == 0, high[:, None],
        jnp.where(place == 1, mid[:, None], jnp.where(place == 2, rest[:, None], 0.0)),
    )
    scale_cols = jnp.broadcast_to(split.reshape(held_rows, 1), (held_rows, LANES)).astype(jnp.bfloat16)
    up_wide = jnp.concatenate([up_rows, scale_cols], axis=1)
    lane = jnp.arange(LANES, dtype=jnp.int32)[None, :]
    key = stored[:, None] - (lane >= rank).astype(jnp.int32)
    bf16, f32 = jnp.bfloat16, jnp.float32
    hops = (2, depth - 1, PARTS)
    any_spec = pl.BlockSpec(memory_space=pl.ANY)
    vmem = pl.BlockSpec(memory_space=pltpu.VMEM)
    return pl.pallas_call(
        functools.partial(kernel, depth),
        out_shape=jax.ShapeDtypeStruct((rows, outs), bf16),
        in_specs=[any_spec] * 4 + [vmem],
        out_specs=vmem,
        scratch_shapes=[
            pltpu.VMEM((rows, feats), bf16),
            pltpu.VMEM((feats, outs), bf16),
            pltpu.VMEM((2, feats, outs // 2), bf16),
            pltpu.VMEM((2 * depth, held_rows, feats + outs + LANES), bf16),
            pltpu.VMEM((rows, outs), f32),
            pltpu.VMEM((2, rows, outs // 2), bf16),
            pltpu.VMEM((2, rows, outs // 2), bf16),
            pltpu.VMEM((rows, LANES), f32),
            pltpu.VMEM((rows, LANES), f32),
            pltpu.VMEM((rows // 2, LANES), f32),
            pltpu.VMEM((rows // 2, LANES), f32),
            pltpu.SemaphoreType.DMA((4,)),
            pltpu.SemaphoreType.DMA(hops),
            pltpu.SemaphoreType.DMA(hops),
            pltpu.SemaphoreType.DMA(hops),
            pltpu.SemaphoreType.DMA(hops),
            pltpu.SemaphoreType.DMA(hops + (2,)),
            pltpu.SemaphoreType.DMA(hops + (2,)),
            pltpu.SemaphoreType.DMA((8,)),
            pltpu.SemaphoreType.DMA((8,)),
        ],
        compiler_params=pltpu.CompilerParams(
            collective_id=0, has_side_effects=True, vmem_limit_bytes=58 * 1024 * 1024
        ),
    )(tokens, base, down_rows, up_wide, key)


def plain(tokens, stored, base, down_rows, up_rows, scale_rows, adapters):
    rows = tokens.shape[0]
    rank = down_rows.shape[0] // scale_rows.shape[0]
    owners = ("adapters", "sub")
    down_all = lax.all_gather(down_rows, owners, axis=0, tiled=True)
    up_all = lax.all_gather(up_rows, owners, axis=0, tiled=True)
    scale_all = lax.all_gather(scale_rows, owners, axis=0, tiled=True)
    base_rows = lax.all_to_all(base, "tp", split_axis=0, concat_axis=1, tiled=True)
    base_sum = lax.psum_scatter(
        jnp.dot(tokens, base_rows, preferred_element_type=jnp.float32),
        "tp", scatter_dimension=1, tiled=True,
    )
    one_hot = stored[:, None] == jnp.arange(adapters, dtype=jnp.int32)[None, :]
    wide = lax.dot_general(
        tokens, down_all, (((1,), (1,)), ((), ())), preferred_element_type=jnp.float32
    )
    low = jnp.sum(jnp.where(one_hot[:, :, None], wide.reshape(rows, adapters, rank), 0.0), axis=1)
    low = lax.psum(low, "tp").astype(jnp.bfloat16)
    spread = jnp.where(one_hot[:, :, None], low[:, None, :], 0).reshape(rows, adapters * rank)
    delta = jnp.dot(spread, up_all, preferred_element_type=jnp.float32)
    scale = jnp.sum(jnp.where(one_hot, scale_all[None, :], 0.0), axis=1)
    delta = (delta * scale[:, None]).astype(jnp.bfloat16)
    return (base_sum + delta.astype(jnp.float32)).astype(jnp.bfloat16)


def local(
    sizes, tokens, token_adapter_index, adapter_slot_table, base, down, up, scale_rows
):
    held, feats, rank = down.shape
    adapters = adapter_slot_table.shape[0]
    outs = base.shape[1]
    slots = jnp.arange(adapters, dtype=jnp.int32)
    named = token_adapter_index == slots[None, :]
    stored = jnp.sum(jnp.where(named, adapter_slot_table[None, :], 0), axis=1)
    down_rows = jnp.swapaxes(down, 1, 2).reshape(held * rank, feats)
    up_rows = up.reshape(held * rank, outs)
    depth = sizes["adapters"]
    small = sizes["groups"] == sizes["tp"] == sizes["sub"] == 2 and 2 <= depth <= 4
    if small and held == 4 and 2 * rank == LANES:
        return fused(depth, tokens, stored, base, down_rows, up_rows, scale_rows)
    return plain(tokens, stored, base, down_rows, up_rows, scale_rows, adapters)


def solution(mesh):
    in_specs = (
        P(("groups", "adapters", "sub"), "tp"),
        P(("groups", "adapters", "sub"), None),
        P(),
        P(None, "tp"),
        P(("adapters", "sub"), "tp", None),
        P(("adapters", "sub"), None, "tp"),
        P(("adapters", "sub")),
    )
    out_specs = P(("groups", "adapters", "sub"), "tp")
    return jax.shard_map(
        functools.partial(local, dict(mesh.shape)), mesh=mesh,
        in_specs=in_specs, out_specs=out_specs, check_vma=False,
    )
```

```python
import functools

import jax
import jax.numpy as jnp
from jax import lax
from jax.experimental import pallas as pl
from jax.experimental.pallas import tpu as pltpu
from jax.sharding import PartitionSpec as P

LANES = 128
PARTS = 4


def kernel(
    depth,
    tok_hbm, base_hbm, down_hbm, up_hbm, named_ref, table_ref, scale_ref,
    out_ref,
    tok, wmine, wcross, buf, ups, scales, key_ref, acc, pout, pin, lacc, lpo, lpi,
    local_sem, send_z, recv_z, send_y, recv_y, send_c, recv_c, send_x, recv_x,
):
    rows, feats = tok.shape
    held_rows = buf.shape[1]
    outs = wmine.shape[1]
    half_outs = outs // 2
    half_feats = feats // 2
    half = held_rows // 2
    step_rows = half // PARTS
    tile = rows // 2
    spots = tile // 2
    ups_part, scale_part = PARTS, PARTS + 1
    g = lax.axis_index("groups")
    z = lax.axis_index("adapters")
    p = lax.axis_index("tp")
    s = lax.axis_index("sub")
    me = 2 * z + s

    def remote(src, dst, send, recv, to):
        return pltpu.make_async_remote_copy(
            src_ref=src, dst_ref=dst, send_sem=send, recv_sem=recv,
            device_id=to, device_id_type=pl.DeviceIdType.MESH,
        )

    def piece(owner, h, q):
        if q == scale_part:
            return scales.at[owner]
        if q == ups_part:
            return ups.at[owner, pl.ds(pl.multiple_of(h * half, half), half)]
        start = pl.multiple_of(h * half + q * step_rows, step_rows)
        return buf.at[owner, pl.ds(start, step_rows)]

    def source(d, k):
        return z - k if d == 0 else z + k

    def exists(d, k):
        return z >= k if d == 0 else z + k < depth

    def can_send(d):
        return z + 1 < depth if d == 0 else z >= 1

    x_to, y_to, c_to = {"tp": 1 - p}, {"groups": 1 - g}, {"sub": 1 - s}

    def z_copy(d, k, q):
        block = piece(2 * source(d, k) + s, g, q)
        to = {"adapters": z + 1 if d == 0 else z - 1}
        first = block
        if k == 0 and q < PARTS:
            first = down_hbm.at[pl.ds(pl.multiple_of(g * half + q * step_rows, step_rows), step_rows)]
        elif k == 0 and q == ups_part:
            first = up_hbm.at[pl.ds(pl.multiple_of(g * half, half), half)]
        return remote(first, block, send_z.at[d, k, q], recv_z.at[d, k, q], to)

    def z_arrival(d, k, q):
        block = piece(2 * source(d, k + 1) + s, g, q)
        return remote(block, block, send_z.at[d, k, q], recv_z.at[d, k, q], x_to)

    def y_copy(d, k, q, h):
        block = piece(2 * source(d, k + 1) + s, h, q)
        return remote(block, block, send_y.at[d, k, q], recv_y.at[d, k, q], y_to)

    def c_copy(d, k, q, w, core):
        block = piece(2 * source(d, k + 1) + core, g if w == 0 else 1 - g, q)
        return remote(block, block, send_c.at[d, k, q, w], recv_c.at[d, k, q, w], c_to)

    def own_copies(core):
        owner = 2 * z + core
        return [
            remote(down_hbm, buf.at[owner], send_x.at[0], recv_x.at[0], c_to),
            remote(up_hbm, ups.at[owner], send_x.at[9], recv_x.at[9], c_to),
            remote(scales.at[owner], scales.at[owner], send_x.at[10], recv_x.at[10], c_to),
        ]

    def x_copy(c):
        first = pl.multiple_of((1 - p) * feats + s * half_feats, half_feats)
        return remote(
            base_hbm.at[pl.ds(first, half_feats), pl.ds(c * half_outs, half_outs)],
            wcross.at[c, pl.ds(pl.multiple_of(s * half_feats, half_feats), half_feats)],
            send_x.at[1 + c], recv_x.at[1 + c], x_to,
        )

    def xc_copy(c, core):
        block = wcross.at[c, pl.ds(pl.multiple_of(core * half_feats, half_feats), half_feats)]
        return remote(block, block, send_x.at[3 + c], recv_x.at[3 + c], c_to)

    def part_copy(c):
        return remote(pout.at[c], pin.at[c], send_x.at[5 + c], recv_x.at[5 + c], x_to)

    def low_copy(b):
        return remote(lpo.at[b], lpi.at[b], send_x.at[7 + b], recv_x.at[7 + b], x_to)

    loads = [
        pltpu.make_async_copy(down_hbm, buf.at[me], local_sem.at[0]),
        pltpu.make_async_copy(up_hbm, ups.at[me], local_sem.at[1]),
        pltpu.make_async_copy(tok_hbm, tok, local_sem.at[2]),
        pltpu.make_async_copy(
            base_hbm.at[pl.ds(pl.multiple_of(p * feats, feats), feats)], wmine, local_sem.at[3]
        ),
    ]
    for load in loads:
        load.start()

    lane = lax.broadcasted_iota(jnp.int32, (1, LANES), 1)
    for h in range(2):
        scales[me, pl.ds(h, 1)] = jnp.where(lane < LANES // 2, scale_ref[2 * h], scale_ref[2 * h + 1])

    barrier = pltpu.get_barrier_semaphore()
    for to in (x_to, y_to, c_to):
        pl.semaphore_signal(barrier, inc=1, device_id=to, device_id_type=pl.DeviceIdType.MESH)
    for d in range(2):
        @pl.when(can_send(d))
        def _(d=d):
            to = {"adapters": z + 1 if d == 0 else z - 1}
            pl.semaphore_signal(barrier, inc=1, device_id=to, device_id_type=pl.DeviceIdType.MESH)
    pl.semaphore_wait(barrier, 3 + (z >= 1).astype(jnp.int32) + (z + 1 < depth).astype(jnp.int32))

    for c in range(2):
        x_copy(c).start()
    for q in (*range(PARTS), ups_part, scale_part):
        for d in range(2):
            @pl.when(can_send(d))
            def _(d=d, q=q):
                z_copy(d, 0, q).start()
    for copy in own_copies(s):
        copy.start()

    def project_tile(owner, i):
        at = pl.ds(pl.multiple_of(i * tile, tile), tile)
        wide = lax.dot_general(
            tok[at], buf[owner], (((1,), (1,)), ((), ())), preferred_element_type=jnp.float32
        )
        key = key_ref[at]
        lacc[at] += jnp.where(key == 4 * owner, wide[:, :LANES], 0.0) + jnp.where(
            key == 4 * owner + 2, wide[:, LANES:], 0.0
        )

    def project(owner):
        @pl.loop(0, 2)
        def _(i):
            project_tile(owner, i)

    def z_events(k, q):
        for d in range(2):
            @pl.when(exists(d, k + 1))
            def _(d=d):
                z_arrival(d, k, q).wait_recv()
                if k + 1 < depth - 1:
                    @pl.when(can_send(d))
                    def _():
                        z_copy(d, k + 1, q).start()
                if q != scale_part:
                    y_copy(d, k, q, g).start()
                c_copy(d, k, q, 0, s).start()

    def y_events(k, q):
        for d in range(2):
            @pl.when(exists(d, k + 1))
            def _(d=d):
                y_copy(d, k, q, 1 - g).wait_recv()
                c_copy(d, k, q, 1, s).start()

    def arrived(d, k, parts):
        @pl.when(exists(d, k + 1))
        def _():
            for q in parts:
                for w in range(1 if q == scale_part else 2):
                    c_copy(d, k, q, w, 1 - s).wait_recv()

    def owners(d, k):
        arrived(d, k, range(PARTS))

        @pl.when(exists(d, k + 1))
        def _():
            @pl.loop(0, 2)
            def _(core):
                project(2 * source(d, k + 1) + core)

    def take_cross(c):
        x_copy_in = remote(
            wcross.at[c, pl.ds(pl.multiple_of(s * half_feats, half_feats), half_feats)],
            wcross.at[c, pl.ds(pl.multiple_of(s * half_feats, half_feats), half_feats)],
            send_x.at[1 + c], recv_x.at[1 + c], x_to,
        )
        x_copy_in.wait_recv()
        xc_copy(c, s).start()

    def cross(c):
        xc_copy(c, 1 - s).wait_recv()

        @pl.loop(0, rows // tile)
        def _(i):
            at = pl.ds(pl.multiple_of(i * tile, tile), tile)
            pout[c, at] = jnp.dot(
                tok[at], wcross[c], preferred_element_type=jnp.float32
            ).astype(jnp.bfloat16)

        part_copy(c).start()

    named = named_ref[...]
    stored = jnp.zeros_like(named)
    for a in range(table_ref.shape[0]):
        stored += jnp.where(named == a, table_ref[a], 0)
    stored = stored.astype(jnp.float32)
    for n in range(rows // LANES):
        square = jnp.broadcast_to(stored[n : n + 1], (LANES, LANES)).T.astype(jnp.int32)
        key_ref[pl.ds(n * LANES, LANES)] = square - (lane >= LANES // 2).astype(jnp.int32)
    lacc[...] = jnp.zeros_like(lacc)
    for load in loads[:3]:
        load.wait()
    project(me)
    loads[3].wait()

    @pl.loop(0, rows // tile)
    def _(i):
        at = pl.ds(pl.multiple_of(i * tile, tile), tile)
        for c in range(2):
            cols = pl.ds(c * half_outs, half_outs)
            acc[at, cols] = jnp.dot(tok[at], wmine[:, cols], preferred_element_type=jnp.float32)

    def sibling():
        own_copies(1 - s)[0].wait_recv()
        project(2 * z + 1 - s)

    steps = (depth - 1) * PARTS
    tasks = {1: [sibling], 3: [lambda: take_cross(0)], 4: [lambda: cross(0)],
             7: [lambda: take_cross(1)], 8: [lambda: cross(1)]}
    last = depth - 2
    for k in range(last):
        tasks.setdefault(k * PARTS + PARTS + 1, []).append(lambda k=k: owners(0, k))
        tasks.setdefault(k * PARTS + PARTS + 2, []).append(lambda k=k: owners(1, k))
    for i in range(max(steps, max(tasks)) + 1):
        if i < steps:
            z_events(i // PARTS, i % PARTS)
        if 0 < i <= steps:
            y_events((i - 1) // PARTS, (i - 1) % PARTS)
        for task in tasks.get(i, []):
            task()

    for k in range(last):
        for q in (ups_part, scale_part):
            z_events(k, q)
    for d in range(2):
        arrived(d, last, range(PARTS))
    low_lane = lax.broadcasted_iota(jnp.int32, (spots, LANES), 1) < LANES // 2
    for b in range(2):
        for d in range(2):
            @pl.when(exists(d, last + 1))
            def _(d=d, b=b):
                @pl.loop(0, 2)
                def _(core):
                    project_tile(2 * source(d, last + 1) + core, b)

        part = lacc[pl.ds(b * tile, tile)]
        folded = part + pltpu.roll(part, LANES // 2, 1)
        lpo[b] = jnp.where(low_lane, folded[:spots], folded[spots:])
        low_copy(b).start()
        if b == 0:
            for q in (ups_part, scale_part):
                z_events(last, q)
    for k in range(depth - 1):
        y_events(k, ups_part)
    for c in range(2):
        part_copy(c).wait_recv()
    for copy in own_copies(1 - s)[1:]:
        copy.wait_recv()
    for k in range(depth - 1):
        for d in range(2):
            arrived(d, k, (ups_part, scale_part))

    end_tile = min(256, spots)
    for b in range(2):
        low_copy(b).wait_recv()
        both = lpo[b] + lpi[b]
        turned = pltpu.roll(both, LANES // 2, 1)
        lacc[pl.ds(b * tile, spots)] = jnp.where(low_lane, both, turned)
        lacc[pl.ds(b * tile + spots, spots)] = jnp.where(low_lane, turned, both)

        @pl.loop(0, tile // end_tile)
        def _(i, b=b):
            at = pl.ds(pl.multiple_of(b * tile + i * end_tile, end_tile), end_tile)
            low = lacc[at].astype(jnp.bfloat16).astype(jnp.float32)
            key = key_ref[at]
            scale = jnp.zeros_like(low)
            spread = []
            for j in range(4 * depth):
                mine = key == 2 * j
                scale += jnp.where(mine, scales[j // 2, pl.ds(j % 2, 1)], 0.0)
                spread.append(jnp.where(mine, low, 0.0).astype(jnp.bfloat16))
            spread = jnp.concatenate(spread, axis=1)
            scale += pltpu.roll(scale, LANES // 2, 1)
            for c in range(2):
                cols = pl.ds(c * half_outs, half_outs)
                delta = jnp.dot(
                    spread, ups[:, :, cols].reshape(-1, half_outs), preferred_element_type=jnp.float32
                )
                wide_scale = jnp.concatenate([scale] * (half_outs // LANES), axis=1)
                delta = (delta * wide_scale).astype(jnp.bfloat16).astype(jnp.float32)
                base = acc[at, cols] + pin[c, at].astype(jnp.float32)
                out_ref[at, cols] = (base + delta).astype(jnp.bfloat16)

    for c in range(2):
        x_copy(c).wait_send()
        xc_copy(c, s).wait_send()
        part_copy(c).wait_send()
    for b in range(2):
        low_copy(b).wait_send()
    for copy in own_copies(s):
        copy.wait_send()
    for k in range(depth - 1):
        for d in range(2):
            @pl.when(exists(d, k) & can_send(d))
            def _(d=d, k=k):
                for q in range(PARTS + 2):
                    z_copy(d, k, q).wait_send()

            @pl.when(exists(d, k + 1))
            def _(d=d, k=k):
                for q in range(PARTS + 2):
                    c_copy(d, k, q, 0, s).wait_send()
                    if q != scale_part:
                        y_copy(d, k, q, g).wait_send()
                        c_copy(d, k, q, 1, s).wait_send()


def fused(depth, tokens, named, table, base, down_rows, up_rows, scale_rows):
    rows, feats = tokens.shape
    held_rows, outs = up_rows.shape
    bf16, f32 = jnp.bfloat16, jnp.float32
    hops = (2, depth - 1, PARTS + 2)
    any_spec = pl.BlockSpec(memory_space=pl.ANY)
    vmem = pl.BlockSpec(memory_space=pltpu.VMEM)
    smem = pl.BlockSpec(memory_space=pltpu.SMEM)
    return pl.pallas_call(
        functools.partial(kernel, depth),
        out_shape=jax.ShapeDtypeStruct((rows, outs), bf16),
        in_specs=[any_spec] * 4 + [vmem, smem, smem],
        out_specs=vmem,
        scratch_shapes=[
            pltpu.VMEM((rows, feats), bf16),
            pltpu.VMEM((feats, outs), bf16),
            pltpu.VMEM((2, feats, outs // 2), bf16),
            pltpu.VMEM((2 * depth, held_rows, feats), bf16),
            pltpu.VMEM((2 * depth, held_rows, outs), bf16),
            pltpu.VMEM((2 * depth, 8, LANES), f32),
            pltpu.VMEM((rows, LANES), jnp.int32),
            pltpu.VMEM((rows, outs), f32),
            pltpu.VMEM((2, rows, outs // 2), bf16),
            pltpu.VMEM((2, rows, outs // 2), bf16),
            pltpu.VMEM((rows, LANES), f32),
            pltpu.VMEM((2, rows // 4, LANES), f32),
            pltpu.VMEM((2, rows // 4, LANES), f32),
            pltpu.SemaphoreType.DMA((4,)),
            pltpu.SemaphoreType.DMA(hops),
            pltpu.SemaphoreType.DMA(hops),
            pltpu.SemaphoreType.DMA(hops),
            pltpu.SemaphoreType.DMA(hops),
            pltpu.SemaphoreType.DMA(hops + (2,)),
            pltpu.SemaphoreType.DMA(hops + (2,)),
            pltpu.SemaphoreType.DMA((11,)),
            pltpu.SemaphoreType.DMA((11,)),
        ],
        compiler_params=pltpu.CompilerParams(
            collective_id=0, has_side_effects=True, vmem_limit_bytes=58 * 1024 * 1024
        ),
    )(tokens, base, down_rows, up_rows, named.reshape(rows // LANES, LANES), table, scale_rows)


def plain(tokens, stored, base, down_rows, up_rows, scale_rows, adapters):
    rows = tokens.shape[0]
    rank = down_rows.shape[0] // scale_rows.shape[0]
    owners = ("adapters", "sub")
    down_all = lax.all_gather(down_rows, owners, axis=0, tiled=True)
    up_all = lax.all_gather(up_rows, owners, axis=0, tiled=True)
    scale_all = lax.all_gather(scale_rows, owners, axis=0, tiled=True)
    base_rows = lax.all_to_all(base, "tp", split_axis=0, concat_axis=1, tiled=True)
    base_sum = lax.psum_scatter(
        jnp.dot(tokens, base_rows, preferred_element_type=jnp.float32),
        "tp", scatter_dimension=1, tiled=True,
    )
    one_hot = stored[:, None] == jnp.arange(adapters, dtype=jnp.int32)[None, :]
    wide = lax.dot_general(
        tokens, down_all, (((1,), (1,)), ((), ())), preferred_element_type=jnp.float32
    )
    low = jnp.sum(jnp.where(one_hot[:, :, None], wide.reshape(rows, adapters, rank), 0.0), axis=1)
    low = lax.psum(low, "tp").astype(jnp.bfloat16)
    spread = jnp.where(one_hot[:, :, None], low[:, None, :], 0).reshape(rows, adapters * rank)
    delta = jnp.dot(spread, up_all, preferred_element_type=jnp.float32)
    scale = jnp.sum(jnp.where(one_hot, scale_all[None, :], 0.0), axis=1)
    delta = (delta * scale[:, None]).astype(jnp.bfloat16)
    return (base_sum + delta.astype(jnp.float32)).astype(jnp.bfloat16)


def local(
    sizes, tokens, token_adapter_index, adapter_slot_table, base, down, up, scale_rows
):
    held, feats, rank = down.shape
    adapters = adapter_slot_table.shape[0]
    outs = base.shape[1]
    down_rows = jnp.swapaxes(down, 1, 2).reshape(held * rank, feats)
    up_rows = up.reshape(held * rank, outs)
    depth = sizes["adapters"]
    small = sizes["groups"] == sizes["tp"] == sizes["sub"] == 2 and 2 <= depth <= 4
    if small and held == 4 and 2 * rank == LANES:
        return fused(
            depth, tokens, token_adapter_index, adapter_slot_table, base, down_rows, up_rows, scale_rows
        )
    slots = jnp.arange(adapters, dtype=jnp.int32)
    named = token_adapter_index == slots[None, :]
    stored = jnp.sum(jnp.where(named, adapter_slot_table[None, :], 0), axis=1)
    return plain(tokens, stored, base, down_rows, up_rows, scale_rows, adapters)


def solution(mesh):
    in_specs = (
        P(("groups", "adapters", "sub"), "tp"),
        P(("groups", "adapters", "sub"), None),
        P(),
        P(None, "tp"),
        P(("adapters", "sub"), "tp", None),
        P(("adapters", "sub"), None, "tp"),
        P(("adapters", "sub")),
    )
    out_specs = P(("groups", "adapters", "sub"), "tp")
    return jax.shard_map(
        functools.partial(local, dict(mesh.shape)), mesh=mesh,
        in_specs=in_specs, out_specs=out_specs, check_vma=False,
    )
```
